32 devices in a mesh: ctx: 16 (over z, y, x), shard: 2 (over core).
Axes of the slice: x: 2, y: 2, z: 4, core: 2. Of those that a mesh axis runs over, the one named last changes fastest.
Arguments:
- inputs: bfloat16 [2, 4608, 768], P('shard', 'ctx'), may hold values from -6 to 6
- cotangent: bfloat16 [2, 4608, 768], P('shard', 'ctx'), may hold values from -6 to 6
- block_table: int32 [16, 2], replicated, may hold values from 0 to 31, as said below
- first_gain: bfloat16 [768], P('shard'), may hold values from 0.5 to 1.5
- first_shift: bfloat16 [768], P('shard'), may hold values from -0.59765625 to 0.59765625
- query_weight: bfloat16 [768, 768], P('shard'), may hold values from -0.4375 to 0.4375
- query_bias: bfloat16 [768], P('shard'), may hold values from -0.59765625 to 0.59765625
- keyvalue_weight: bfloat16 [768, 1536], P('shard'), may hold values from -0.21875 to 0.21875
- value_bias: bfloat16 [768], P('shard'), may hold values from -0.29882812 to 0.29882812
- out_weight: bfloat16 [768, 768], P('shard'), may hold values from -1.75 to 1.75
- out_bias: bfloat16 [768], P('shard'), may hold values from -0.59765625 to 0.59765625
- second_gain: bfloat16 [768], P('shard'), may hold values from 0.5 to 1.5
- second_shift: bfloat16 [768], P('shard'), may hold values from -0.59765625 to 0.59765625
- up_weight: bfloat16 [768, 3072], P('shard'), may hold values from -0.21875 to 0.21875
- up_bias: bfloat16 [3072], P('shard'), may hold values from -0.59765625 to 0.59765625
- down_weight: bfloat16 [3072, 768], P('shard'), may hold values from -0.109375 to 0.109375
- down_bias: bfloat16 [768], P('shard'), may hold values from -0.59765625 to 0.59765625
Outputs:
- outputs: bfloat16 [2, 4608, 768], P('shard', 'ctx')
- input_grad: bfloat16 [2, 4608, 768], P('shard', 'ctx')
- first_gain_grad: float32 [768], P('shard')
- first_shift_grad: float32 [768], P('shard')
- query_weight_grad: float32 [768, 768], P('shard')
- query_bias_grad: float32 [768], P('shard')
- keyvalue_weight_grad: float32 [768, 1536], P('shard')
- value_bias_grad: float32 [768], P('shard')
- out_weight_grad: float32 [768, 768], P('shard')
- out_bias_grad: float32 [768], P('shard')
- second_gain_grad: float32 [768], P('shard')
- second_shift_grad: float32 [768], P('shard')
- up_weight_grad: float32 [768, 3072], P('shard')
- up_bias_grad: float32 [3072], P('shard')
- down_weight_grad: float32 [3072, 768], P('shard')
- down_bias_grad: float32 [768], P('shard')
The draws below stay inside these ranges and needn't reach their ends.
Inputs may be any that keep to these rules, and one draw needn't show every extreme that they name: `block_table`: row d holds a block number b and its mirror 32 - 1 - b, in either order; every block number stands once in the table.
All inputs are finite; a program needn't handle non-finite values.
Results may differ from the reference program's by a relative error of at most 0.017.
Values may be sent and summed in bfloat16 or wider, within the bound.
A program may use at most 512 MiB of HBM per device.

```python
import math
import jax
import jax.numpy as jnp
from jax import lax

D = 768
HD = 64
FF = 3072
BLOCKS = 32
LEN = 4608
SEQS = 2


def draw_block_table(key, part):
    key = jax.random.fold_in(key, 7)
    key_order, key_flip = jax.random.split(key)
    pair_count = BLOCKS // 2
    chosen = jax.random.permutation(key_order, pair_count).astype(jnp.int32)
    flipped = jax.random.randint(key_flip, (pair_count,), 0, 2)
    mirror = BLOCKS - 1 - chosen
    first_col = jnp.where(flipped == 1, mirror, chosen)
    second_col = jnp.where(flipped == 1, chosen, mirror)
    return jnp.stack([first_col, second_col], 1).astype(jnp.int32)


def steps_of(stream_key, extent, cuts, least, top_value):
    factor_of, own = 1.0, jax.random.fold_in(stream_key, 6)
    for axis_at, parts in cuts:
        draws = jnp.exp(jax.random.uniform(jax.random.fold_in(own, axis_at), (parts,), jnp.float32, least / len(cuts), top_value / len(cuts)))
        factor_of = factor_of * jnp.repeat(draws, extent[axis_at] // parts).reshape([-1 if axis == axis_at else 1 for axis in range(len(extent))])
    return factor_of


def scatter_about(key, extent, deviation, reach, cuts=(), kind=jnp.bfloat16):
    result = jax.random.normal(key, extent, jnp.float32) * deviation
    if len(cuts) > 0:
        result = steps_of(key, extent, cuts, -0.22, 0.18) * result
    return jnp.clip(result, min=-reach, max=reach).astype(kind)


def setup_inputs(seed: int = 0) -> dict:
    arg_keys = jax.random.split(jax.random.key(seed), 18)
    return {
        "inputs": scatter_about(arg_keys[0], (SEQS, LEN, D), 1.0, 6.0, ((0, 2), (1, 16))),
        "cotangent": scatter_about(arg_keys[1], (SEQS, LEN, D), 1.0, 6.0, ((0, 2), (1, 16))),
        "block_table": draw_block_table(jax.random.fold_in(arg_keys[17], 71), 0),
        "first_gain": jnp.clip(1.0 + 0.1 * jax.random.normal(arg_keys[3], (D,), jnp.float32), 0.5, 1.5).astype(jnp.bfloat16),
        "first_shift": scatter_about(arg_keys[4], (D,), 0.1, 0.59765625, ((0, 2),)),
        "query_weight": scatter_about(arg_keys[5], (D, D), (D // 4) ** -0.5, 0.4375, ((0, 2),)),
        "query_bias": scatter_about(arg_keys[6], (D,), 0.1, 0.59765625, ((0, 2),)),
        "keyvalue_weight": scatter_about(arg_keys[7], (D, 2 * D), D ** -0.5, 0.21875, ((0, 2),)),
        "value_bias": scatter_about(arg_keys[8], (D,), 0.05, 0.29882812, ((0, 2),)),
        "out_weight": scatter_about(arg_keys[9], (D, D), (D // 64) ** -0.5, 1.75, ((0, 2),)),
        "out_bias": scatter_about(arg_keys[10], (D,), 0.1, 0.59765625, ((0, 2),)),
        "second_gain": jnp.clip(1.0 + 0.1 * jax.random.normal(arg_keys[11], (D,), jnp.float32), 0.5, 1.5).astype(jnp.bfloat16),
        "second_shift": scatter_about(arg_keys[12], (D,), 0.1, 0.59765625, ((0, 2),)),
        "up_weight": scatter_about(arg_keys[13], (D, FF), D ** -0.5, 0.21875, ((0, 2),)),
        "up_bias": scatter_about(arg_keys[14], (FF,), 0.1, 0.59765625, ((0, 2),)),
        "down_weight": scatter_about(arg_keys[15], (FF, D), FF ** -0.5, 0.109375, ((0, 2),)),
        "down_bias": scatter_about(arg_keys[16], (D,), 0.1, 0.59765625, ((0, 2),)),
    }


@jax.custom_vjp
def low(v):
    return lax.optimization_barrier(v.astype(jnp.bfloat16)).astype(jnp.float32)

@jax.custom_vjp
def low_back(v):
    return v

def low_keep(v):
    return (low(v), None)

def low_pass(kept, grad):
    return (grad,)

def back_keep(v):
    return (v, None)

def back_low(kept, grad):
    return (low(grad),)
low.defvjp(low_keep, low_pass)
low_back.defvjp(back_keep, back_low)
EPSILON = 1e-05
NEGATIVE = -1e+30

def normalize(values, gain, shift):
    centre = values - lax.optimization_barrier(jnp.mean(values, -1, keepdims=True))
    spread = lax.optimization_barrier(jnp.mean(centre * centre, -1, keepdims=True))
    return centre * lax.rsqrt(spread + EPSILON) * gain + shift

def product(left, right):
    return jnp.dot(left, right, precision=lax.Precision.HIGHEST)

def attention(queries, keys_all, values_all):
    length = queries.shape[0]
    block_rows = math.gcd(length, 512)
    head_count = queries.shape[1] // HD
    query_blocks = queries.reshape(length // block_rows, block_rows, head_count, HD)
    key_heads = keys_all.reshape(length, head_count, HD)
    value_heads = values_all.reshape(length, head_count, HD)
    key_places = jnp.arange(length, dtype=jnp.int32)
    first_rows = jnp.arange(length // block_rows, dtype=jnp.int32) * block_rows

    def one_block(pieces):
        query_block, first_row = pieces
        scores = low_back(jnp.einsum('qhd,khd->hqk', query_block, key_heads, precision=lax.Precision.HIGHEST))
        places = first_row + jnp.arange(block_rows, dtype=jnp.int32)
        allowed = places[:, None] >= key_places[None, :]
        scores = jnp.where(allowed[None], scores, NEGATIVE)
        largest = lax.optimization_barrier(jnp.max(scores, -1, keepdims=True))
        expo = jnp.exp(scores - largest)
        probability = low(expo / lax.optimization_barrier(jnp.sum(expo, -1, keepdims=True)))
        return jnp.einsum('hqk,khd->qhd', probability, value_heads, precision=lax.Precision.HIGHEST)
    attended = lax.map(jax.checkpoint(one_block), (query_blocks, first_rows))
    return attended.reshape(length, head_count * HD)

def layer(inputs, first_gain, first_shift, query_weight, query_bias, keyvalue_weight, value_bias, out_weight, out_bias, second_gain, second_shift, up_weight, up_bias, down_weight, down_bias):
    model_width = inputs.shape[-1]
    kv_shift = jnp.concatenate([jnp.zeros_like(value_bias), value_bias])

    def one_sequence(hidden):
        normed = low(normalize(hidden, first_gain, first_shift))
        queries = low(low_back((product(normed, query_weight) + query_bias) * 0.125))
        keyvalue = low(low_back(product(normed, keyvalue_weight) + kv_shift))
        attended = low(low_back(attention(queries, keyvalue[:, :model_width], keyvalue[:, model_width:])))
        middle = hidden + low_back(product(attended, out_weight) + out_bias)
        second = low(normalize(middle, second_gain, second_shift))
        pre_act = low_back(product(second, up_weight) + up_bias)
        active = low(jax.nn.gelu(pre_act, approximate=True))
        return middle + low_back(product(active, down_weight) + down_bias)
    return lax.map(one_sequence, inputs)

def reference(inputs, cotangent, block_table, first_gain, first_shift, query_weight, query_bias, keyvalue_weight, value_bias, out_weight, out_bias, second_gain, second_shift, up_weight, up_bias, down_weight, down_bias):
    dealt_order = block_table.reshape(-1).astype(jnp.int32)
    inverse = jnp.argsort(dealt_order).astype(jnp.int32)
    seq_count, length, model_width = inputs.shape
    block_count = dealt_order.shape[0]

    def to_sequence(values):
        blocks = values.reshape(seq_count, block_count, length // block_count, model_width)
        return blocks[:, inverse].reshape(seq_count, length, model_width)

    def to_dealt(values):
        blocks = values.reshape(seq_count, block_count, length // block_count, model_width)
        return blocks[:, dealt_order].reshape(seq_count, length, model_width)
    params = tuple((param_arg.astype(jnp.float32) for param_arg in (first_gain, first_shift, query_weight, query_bias, keyvalue_weight, value_bias, out_weight, out_bias, second_gain, second_shift, up_weight, up_bias, down_weight, down_bias)))
    results, pull = jax.vjp(layer, to_sequence(inputs.astype(jnp.float32)), *params)
    grads = pull(to_sequence(cotangent.astype(jnp.float32)))
    return (to_dealt(results).astype(jnp.bfloat16), to_dealt(grads[0]).astype(jnp.bfloat16), grads[1], grads[2], grads[3], grads[4], grads[5], grads[6], grads[7], grads[8], grads[9], grads[10], grads[11], grads[12], grads[13], grads[14])
```

```python
import jax
import jax.numpy as jnp
from jax import lax
from jax.experimental import pallas as pl
from jax.experimental.pallas import tpu as pltpu
from jax.sharding import PartitionSpec as P

HD = 64


EPSILON = 1e-05
NEGATIVE = -1e30


def normalize(values, gain, shift):
    centre = values - jnp.mean(values, -1, keepdims=True)
    spread = jnp.mean(centre * centre, -1, keepdims=True)
    return centre * lax.rsqrt(spread + EPSILON) * gain + shift


def gelu_tanh(values):
    return jax.nn.gelu(values, approximate=True)


def matmul(left, right):
    return jnp.dot(left, right, preferred_element_type=jnp.float32)


def outer_sum(left, right):
    return lax.dot_general(
        left, right, (((0,), (0,)), ((), ())), preferred_element_type=jnp.float32
    )


def times_transpose(left, right):
    return lax.dot_general(
        left, right, (((1,), (1,)), ((), ())), preferred_element_type=jnp.float32
    )


def key_tile_rows(length):
    for rows in (512, 384, 256, 128):
        if length % rows == 0:
            return rows
    return length


def head_halves(rows):
    block_rows, lanes = rows.shape
    lane = lax.broadcasted_iota(jnp.int32, (block_rows, lanes), 1)
    low_mask = (lane < HD).astype(jnp.float32).astype(rows.dtype)
    high_mask = (lane >= HD).astype(jnp.float32).astype(rows.dtype)
    return jnp.concatenate([rows * low_mask, rows * high_mask], 0)


def join_halves(both):
    block_rows = both.shape[0] // 2
    lane = lax.broadcasted_iota(jnp.int32, (block_rows, both.shape[1]), 1)
    return jnp.where(lane < HD, both[:block_rows], both[block_rows:])


def to_sequence(table, block_rows, pairs):
    def move(slot, _):
        source = pl.ds(pl.multiple_of(slot * block_rows, block_rows), block_rows)
        target = pl.ds(pl.multiple_of(table[slot] * block_rows, block_rows), block_rows)
        for dealt, ordered in pairs:
            ordered[target, :] = dealt[source, :]
        return 0

    lax.fori_loop(0, table.shape[0], move, 0)


def allowed_mask(first, block_rows, tile, tile_rows):
    shape = (2 * block_rows, tile_rows)
    row = lax.broadcasted_iota(jnp.int32, shape, 0)
    row = jnp.where(row >= block_rows, row - block_rows, row)
    col = lax.broadcasted_iota(jnp.int32, shape, 1)
    return row - col >= tile * tile_rows - first


def forward_kernel(table, mine, q_ref, k_ref, v_ref, o_ref, lse_ref, k_seq, v_seq):
    block_rows = q_ref.shape[0] // 2
    tile_rows = key_tile_rows(k_ref.shape[0])
    to_sequence(table, block_rows, ((k_ref, k_seq), (v_ref, v_seq)))
    for half in range(2):
        rows = pl.ds(half * block_rows, block_rows)
        queries = head_halves(q_ref[rows, :])
        first = mine[half] * block_rows

        def step(tile, carry, masked):
            running, denominator, total = carry
            place = pl.ds(pl.multiple_of(tile * tile_rows, tile_rows), tile_rows)
            scores = times_transpose(queries, k_seq[place, :])
            if masked:
                scores = jnp.where(
                    allowed_mask(first, block_rows, tile, tile_rows), scores, NEGATIVE
                )
            new_running = jnp.maximum(running, jnp.max(scores, -1, keepdims=True))
            decay = jnp.exp(running - new_running)
            chances = jnp.exp(scores - new_running)
            denominator = denominator * decay + jnp.sum(chances, -1, keepdims=True)
            total = total * decay + matmul(chances.astype(jnp.bfloat16), v_seq[place, :])
            return new_running, denominator, total

        start = (
            jnp.full((2 * block_rows, 1), NEGATIVE, jnp.float32),
            jnp.zeros((2 * block_rows, 1), jnp.float32),
            jnp.zeros((2 * block_rows, q_ref.shape[1]), jnp.float32),
        )
        full = (first + 1) // tile_rows
        count = (first + block_rows - 1) // tile_rows + 1
        carry = lax.fori_loop(0, full, lambda t, c: step(t, c, False), start)
        running, denominator, total = lax.fori_loop(
            full, count, lambda t, c: step(t, c, True), carry
        )
        o_ref[rows, :] = join_halves(total / denominator)
        lse_ref[0, pl.ds(half * 2 * block_rows, 2 * block_rows), :] = jnp.broadcast_to(
            running + jnp.log(denominator), (2 * block_rows, lse_ref.shape[2])
        )


def backward_kernel(
    table, mine, q_ref, do_ref, o_ref, lse_ref, k_ref, v_ref,
    dq_ref, dk_ref, dv_ref, k_seq, v_seq, dk_seq, dv_seq,
):
    block_rows = q_ref.shape[0] // 2
    tile_rows = key_tile_rows(k_ref.shape[0])
    to_sequence(table, block_rows, ((k_ref, k_seq), (v_ref, v_seq)))

    def clear(tile, _):
        place = pl.ds(pl.multiple_of(tile * tile_rows, tile_rows), tile_rows)
        zero = jnp.zeros((tile_rows, dk_seq.shape[1]), jnp.float32)
        dk_seq[place, :] = zero
        dv_seq[place, :] = zero
        return 0

    lax.fori_loop(0, k_ref.shape[0] // tile_rows, clear, 0)
    for half in range(2):
        rows = pl.ds(half * block_rows, block_rows)
        queries = head_halves(q_ref[rows, :])
        grads = head_halves(do_ref[rows, :])
        attended = o_ref[rows, :]
        delta = jnp.sum(
            grads.astype(jnp.float32) * jnp.concatenate([attended, attended], 0), -1, keepdims=True
        )
        log_total = lse_ref[0, pl.ds(half * 2 * block_rows, 2 * block_rows), :][:, :1]
        first = mine[half] * block_rows

        def step(tile, total, masked):
            place = pl.ds(pl.multiple_of(tile * tile_rows, tile_rows), tile_rows)
            keys = k_seq[place, :]
            scores = times_transpose(queries, keys)
            if masked:
                scores = jnp.where(
                    allowed_mask(first, block_rows, tile, tile_rows), scores, NEGATIVE
                )
            chances = jnp.exp(scores - log_total)
            dchance = times_transpose(grads, v_seq[place, :])
            dscores = (chances * (dchance - delta)).astype(jnp.bfloat16)
            dk_seq[place, :] += outer_sum(dscores, queries)
            dv_seq[place, :] += outer_sum(chances.astype(jnp.bfloat16), grads)
            return total + matmul(dscores, keys)

        full = (first + 1) // tile_rows
        count = (first + block_rows - 1) // tile_rows + 1
        total = jnp.zeros((2 * block_rows, q_ref.shape[1]), jnp.float32)
        total = lax.fori_loop(0, full, lambda t, c: step(t, c, False), total)
        total = lax.fori_loop(full, count, lambda t, c: step(t, c, True), total)
        dq_ref[rows, :] = join_halves(total).astype(dq_ref.dtype)

    def back(slot, _):
        target = pl.ds(pl.multiple_of(slot * block_rows, block_rows), block_rows)
        source = pl.ds(pl.multiple_of(table[slot] * block_rows, block_rows), block_rows)
        dk_ref[target, :] = dk_seq[source, :].astype(dk_ref.dtype)
        dv_ref[target, :] = dv_seq[source, :].astype(dv_ref.dtype)
        return 0

    lax.fori_loop(0, table.shape[0], back, 0)


LANES = 2 * HD


def wide_spec(length, shift):
    spare = {} if length <= 8192 else {"pipeline_mode": pl.Buffered(1)}
    return pl.BlockSpec((length, LANES), lambda h, *_: (0, h + shift), **spare)


def attention_cost(length, rows, pairs, products):
    area = rows * length // 2
    return pl.CostEstimate(
        flops=products * 2 * area * LANES * 2 * pairs,
        bytes_accessed=8 * length * LANES * pairs,
        transcendentals=2 * area * pairs,
    )


def attend(queries, kv_all, dealt, mine):
    rows, width = queries.shape
    length = kv_all.shape[0]
    pairs = width // LANES
    small = pl.BlockSpec((rows, LANES), lambda h, *_: (0, h))
    return pl.pallas_call(
        forward_kernel,
        out_shape=(
            jax.ShapeDtypeStruct((rows, width), jnp.float32),
            jax.ShapeDtypeStruct((pairs, 2 * rows, LANES), jnp.float32),
        ),
        grid_spec=pltpu.PrefetchScalarGridSpec(
            num_scalar_prefetch=2,
            grid=(pairs,),
            in_specs=[small, wide_spec(length, 0), wide_spec(length, pairs)],
            out_specs=[small, pl.BlockSpec((1, 2 * rows, LANES), lambda h, *_: (h, 0, 0))],
            scratch_shapes=[pltpu.VMEM((length, LANES), jnp.bfloat16)] * 2,
        ),
        compiler_params=pltpu.CompilerParams(vmem_limit_bytes=(32 if length <= 8192 else 56) << 20),
        cost_estimate=attention_cost(length, rows, pairs, 2),
    )(dealt, mine, queries, kv_all, kv_all)


def attend_back(queries, grads, attended, log_total, kv_all, dealt, mine):
    rows, width = queries.shape
    length = kv_all.shape[0]
    pairs = width // LANES
    small = pl.BlockSpec((rows, LANES), lambda h, *_: (0, h))
    wide = jax.ShapeDtypeStruct((length, width), jnp.bfloat16)
    return pl.pallas_call(
        backward_kernel,
        out_shape=(jax.ShapeDtypeStruct((rows, width), jnp.bfloat16), wide, wide),
        grid_spec=pltpu.PrefetchScalarGridSpec(
            num_scalar_prefetch=2,
            grid=(pairs,),
            in_specs=[
                small,
                small,
                small,
                pl.BlockSpec((1, 2 * rows, LANES), lambda h, *_: (h, 0, 0)),
                wide_spec(length, 0),
                wide_spec(length, pairs),
            ],
            out_specs=[small, wide_spec(length, 0), wide_spec(length, 0)],
            scratch_shapes=[pltpu.VMEM((length, LANES), jnp.bfloat16)] * 2
            + [pltpu.VMEM((length, LANES), jnp.float32)] * 2,
        ),
        compiler_params=pltpu.CompilerParams(vmem_limit_bytes=(32 if length <= 8192 else 60) << 20),
        cost_estimate=attention_cost(length, rows, pairs, 5),
    )(dealt, mine, queries, grads, attended, log_total, kv_all, kv_all)


def gather_vectors(vectors):
    sizes = [v.shape[0] for v in vectors]
    both = lax.all_gather(jnp.concatenate(vectors), "shard", axis=0)
    out, at = [], 0
    for size in sizes:
        out.append(both[:, at : at + size].reshape(-1).astype(jnp.float32))
        at += size
    return out


def sum_vectors(vectors):
    halves = lax.axis_size("shard")
    sizes = [v.shape[0] // halves for v in vectors]
    packed = jnp.concatenate([v.reshape(halves, -1) for v in vectors], 1)
    summed = lax.psum(packed, ("ctx", "shard"))
    here = lax.dynamic_index_in_dim(summed, lax.axis_index("shard"), 0, keepdims=False)
    out, at = [], 0
    for size in sizes:
        out.append(here[at : at + size])
        at += size
    return out


def sum_matrix(term):
    share = lax.psum_scatter(term.astype(jnp.bfloat16), "shard", scatter_dimension=0, tiled=True)
    return lax.psum(share, "ctx").astype(jnp.float32)


def body(
    inputs,
    cotangent,
    block_table,
    first_gain,
    first_shift,
    query_weight,
    query_bias,
    keyvalue_weight,
    value_bias,
    out_weight,
    out_bias,
    second_gain,
    second_shift,
    up_weight,
    up_bias,
    down_weight,
    down_bias,
):
    my_index = lax.axis_index("ctx")
    dealt = block_table.reshape(-1)
    mine = lax.dynamic_index_in_dim(block_table, my_index, 0, keepdims=False)
    gain_one, shift_one, b_query, b_value, b_out, gain_two, shift_two, b_up, b_down = gather_vectors(
        [
            first_gain,
            first_shift,
            query_bias,
            value_bias,
            out_bias,
            second_gain,
            second_shift,
            up_bias,
            down_bias,
        ]
    )
    w_keyvalue = lax.all_gather(keyvalue_weight, "shard", axis=0, tiled=True)
    w_query = lax.all_gather(query_weight, "shard", axis=0, tiled=True)
    w_down = lax.all_gather(down_weight, "shard", axis=0, tiled=True)
    w_out = lax.all_gather(out_weight, "shard", axis=0, tiled=True)
    w_up = lax.all_gather(up_weight, "shard", axis=0, tiled=True)
    kv_shift = jnp.concatenate([jnp.zeros_like(b_value), b_value])
    hidden = inputs[0].astype(jnp.float32)
    normed = normalize(hidden, gain_one, shift_one).astype(jnp.bfloat16)
    kv_local = (matmul(normed, w_keyvalue) + kv_shift).astype(jnp.bfloat16)
    kv_all = lax.all_gather(kv_local, "ctx", axis=0, tiled=True)
    queries = ((matmul(normed, w_query) + b_query) * 0.125).astype(jnp.bfloat16)
    down_grad_in = cotangent[0]
    upstream = down_grad_in.astype(jnp.float32)
    dactive = times_transpose(down_grad_in, w_down)
    attended, log_total = attend(queries, kv_all, dealt, mine)
    attended_low = attended.astype(jnp.bfloat16)
    middle = hidden + matmul(attended_low, w_out) + b_out
    second = normalize(middle, gain_two, shift_two).astype(jnp.bfloat16)
    pre_act = matmul(second, w_up) + b_up
    active = gelu_tanh(pre_act).astype(jnp.bfloat16)
    down_grad = sum_matrix(outer_sum(active, down_grad_in))
    _, gelu_pull = jax.vjp(gelu_tanh, pre_act)
    dpre = gelu_pull(dactive)[0].astype(jnp.bfloat16)
    up_grad = sum_matrix(outer_sum(second, dpre))
    result = middle + matmul(active, w_down) + b_down
    dsecond = times_transpose(dpre, w_up)
    _, norm_pull_two = jax.vjp(normalize, middle, gain_two, shift_two)
    dmiddle_part, dgain_two, dshift_two = norm_pull_two(dsecond)
    dmiddle = upstream + dmiddle_part
    dbranch = dmiddle.astype(jnp.bfloat16)
    dattended = times_transpose(dbranch, w_out).astype(jnp.bfloat16)
    dquery, dkey_all, dvalue_all = attend_back(
        queries, dattended, attended, log_total, kv_all, dealt, mine
    )
    out_grad = sum_matrix(outer_sum(attended_low, dbranch))
    dkey = lax.psum_scatter(dkey_all, "ctx", scatter_dimension=0, tiled=True)
    dvalue = lax.psum_scatter(dvalue_all, "ctx", scatter_dimension=0, tiled=True)
    query_grad = sum_matrix(outer_sum(normed, dquery) * 0.125)
    kv_grad_low = jnp.concatenate([dkey, dvalue], 1)
    keyvalue_grad = sum_matrix(outer_sum(normed, kv_grad_low))
    dnormed = times_transpose(dquery, w_query) * 0.125 + times_transpose(kv_grad_low, w_keyvalue)
    _, norm_pull_one = jax.vjp(normalize, hidden, gain_one, shift_one)
    dhidden_part, dgain_one, dshift_one = norm_pull_one(dnormed)
    input_grad = (dmiddle + dhidden_part).astype(jnp.bfloat16)
    (
        gain_one_grad,
        shift_one_grad,
        query_bias_grad,
        value_bias_grad,
        out_bias_grad,
        gain_two_grad,
        shift_two_grad,
        up_bias_grad,
        down_bias_grad,
    ) = sum_vectors(
        [
            dgain_one,
            dshift_one,
            jnp.sum(dquery.astype(jnp.float32), 0) * 0.125,
            jnp.sum(dvalue.astype(jnp.float32), 0),
            jnp.sum(dbranch.astype(jnp.float32), 0),
            dgain_two,
            dshift_two,
            jnp.sum(dpre.astype(jnp.float32), 0),
            jnp.sum(upstream, 0),
        ]
    )
    return (
        result.astype(jnp.bfloat16)[None],
        input_grad[None],
        gain_one_grad,
        shift_one_grad,
        query_grad,
        query_bias_grad,
        keyvalue_grad,
        value_bias_grad,
        out_grad,
        out_bias_grad,
        gain_two_grad,
        shift_two_grad,
        up_grad,
        up_bias_grad,
        down_grad,
        down_bias_grad,
    )


def solution(mesh):
    in_specs = (
        P("shard", "ctx", None),
        P("shard", "ctx", None),
        P(),
        P("shard"),
        P("shard"),
        P("shard", None),
        P("shard"),
        P("shard", None),
        P("shard"),
        P("shard", None),
        P("shard"),
        P("shard"),
        P("shard"),
        P("shard", None),
        P("shard"),
        P("shard", None),
        P("shard"),
    )
    out_specs = (
        P("shard", "ctx", None),
        P("shard", "ctx", None),
        P("shard"),
        P("shard"),
        P("shard", None),
        P("shard"),
        P("shard", None),
        P("shard"),
        P("shard", None),
        P("shard"),
        P("shard"),
        P("shard"),
        P("shard", None),
        P("shard"),
        P("shard", None),
        P("shard"),
    )
    return jax.shard_map(body, mesh=mesh, in_specs=in_specs, out_specs=out_specs, check_vma=False)
```

```python
import jax
import jax.numpy as jnp
from jax import lax
from jax.experimental import pallas as pl
from jax.experimental.pallas import tpu as pltpu
from jax.sharding import PartitionSpec as P

HD = 64


EPSILON = 1e-05
NEGATIVE = -1e30


def normalize(values, gain, shift):
    centre = values - jnp.mean(values, -1, keepdims=True)
    spread = jnp.mean(centre * centre, -1, keepdims=True)
    return centre * lax.rsqrt(spread + EPSILON) * gain + shift


def gelu_tanh(values):
    return jax.nn.gelu(values, approximate=True)


def matmul(left, right):
    return jnp.dot(left, right, preferred_element_type=jnp.float32)


def outer_sum(left, right):
    return lax.dot_general(
        left, right, (((0,), (0,)), ((), ())), preferred_element_type=jnp.float32
    )


def times_transpose(left, right):
    return lax.dot_general(
        left, right, (((1,), (1,)), ((), ())), preferred_element_type=jnp.float32
    )


def key_tile_rows(length):
    for rows in (512, 384, 256, 128):
        if length % rows == 0:
            return rows
    return length


def stack_heads(rows):
    block_rows, lanes = rows.shape
    head = lax.broadcasted_iota(jnp.int32, (block_rows, lanes), 1) // HD
    parts = [
        rows * (head == h).astype(jnp.float32).astype(rows.dtype) for h in range(lanes // HD)
    ]
    return jnp.concatenate(parts, 0)


def join_heads(stacked):
    lanes = stacked.shape[1]
    block_rows = stacked.shape[0] // (lanes // HD)
    head = lax.broadcasted_iota(jnp.int32, (block_rows, lanes), 1) // HD
    result = stacked[:block_rows]
    for h in range(1, lanes // HD):
        result = jnp.where(head == h, stacked[h * block_rows : (h + 1) * block_rows], result)
    return result


def to_sequence(table, block_rows, pairs):
    def move(slot, _):
        source = pl.ds(pl.multiple_of(slot * block_rows, block_rows), block_rows)
        target = pl.ds(pl.multiple_of(table[slot] * block_rows, block_rows), block_rows)
        for dealt, ordered in pairs:
            ordered[target, :] = dealt[source, :]
        return 0

    lax.fori_loop(0, table.shape[0], move, 0)


def allowed_mask(first, block_rows, heads, tile, tile_rows):
    shape = (block_rows, tile_rows)
    row = lax.broadcasted_iota(jnp.int32, shape, 0)
    col = lax.broadcasted_iota(jnp.int32, shape, 1)
    return jnp.concatenate([row - col] * heads, 0) >= tile * tile_rows - first


def forward_kernel(table, mine, q_ref, k_ref, v_ref, o_ref, lse_ref, k_seq, v_seq):
    block_rows, lanes = q_ref.shape
    heads = lanes // HD
    rows = heads * block_rows
    tile_rows = key_tile_rows(k_ref.shape[0])
    which = pl.program_id(0)

    @pl.when(which == 0)
    def _():
        to_sequence(table, block_rows, ((k_ref, k_seq), (v_ref, v_seq)))

    queries = stack_heads(q_ref[...])
    first = mine[which] * block_rows

    def step(tile, carry, masked):
        running, denominator, total = carry
        place = pl.ds(pl.multiple_of(tile * tile_rows, tile_rows), tile_rows)
        scores = times_transpose(queries, k_seq[place, :])
        if masked:
            allowed = allowed_mask(first, block_rows, heads, tile, tile_rows)
            scores = jnp.where(allowed, scores, NEGATIVE)
        new_running = jnp.maximum(running, jnp.max(scores, -1, keepdims=True))
        decay = jnp.exp(running - new_running)
        chances = jnp.exp(scores - new_running)
        denominator = denominator * decay + jnp.sum(chances, -1, keepdims=True)
        total = total * decay + matmul(chances.astype(jnp.bfloat16), v_seq[place, :])
        return new_running, denominator, total

    start = (
        jnp.full((rows, 1), NEGATIVE, jnp.float32),
        jnp.zeros((rows, 1), jnp.float32),
        jnp.zeros((rows, lanes), jnp.float32),
    )
    full = (first + 1) // tile_rows
    count = (first + block_rows - 1) // tile_rows + 1
    carry = lax.fori_loop(0, full, lambda t, c: step(t, c, False), start)
    running, denominator, total = lax.fori_loop(full, count, lambda t, c: step(t, c, True), carry)
    o_ref[...] = join_heads(total / denominator)
    lse_ref[0] = jnp.broadcast_to(running + jnp.log(denominator), (rows, lse_ref.shape[2]))


def backward_kernel(
    table, mine, q_ref, do_ref, o_ref, lse_ref, k_ref, v_ref,
    dq_ref, dk_ref, dv_ref, k_seq, v_seq, dk_seq, dv_seq,
):
    block_rows, lanes = q_ref.shape
    heads = lanes // HD
    rows = heads * block_rows
    tile_rows = key_tile_rows(k_ref.shape[0])
    which = pl.program_id(0)

    @pl.when(which == 0)
    def _():
        to_sequence(table, block_rows, ((k_ref, k_seq), (v_ref, v_seq)))

        def clear(tile, _):
            place = pl.ds(pl.multiple_of(tile * tile_rows, tile_rows), tile_rows)
            zero = jnp.zeros((tile_rows, lanes), jnp.float32)
            dk_seq[place, :] = zero
            dv_seq[place, :] = zero
            return 0

        lax.fori_loop(0, k_ref.shape[0] // tile_rows, clear, 0)

    queries = stack_heads(q_ref[...])
    grads = stack_heads(do_ref[...])
    delta = jnp.sum(
        grads.astype(jnp.float32) * jnp.concatenate([o_ref[...]] * heads, 0), -1, keepdims=True
    )
    log_total = lse_ref[0][:, :1]
    first = mine[which] * block_rows

    def step(tile, total, masked):
        place = pl.ds(pl.multiple_of(tile * tile_rows, tile_rows), tile_rows)
        keys = k_seq[place, :]
        scores = times_transpose(queries, keys)
        if masked:
            allowed = allowed_mask(first, block_rows, heads, tile, tile_rows)
            scores = jnp.where(allowed, scores, NEGATIVE)
        chances = jnp.exp(scores - log_total)
        dchance = times_transpose(grads, v_seq[place, :])
        dscores = (chances * (dchance - delta)).astype(jnp.bfloat16)
        dk_seq[place, :] += outer_sum(dscores, queries)
        dv_seq[place, :] += outer_sum(chances.astype(jnp.bfloat16), grads)
        return total + matmul(dscores, keys)

    full = (first + 1) // tile_rows
    count = (first + block_rows - 1) // tile_rows + 1
    total = jnp.zeros((rows, lanes), jnp.float32)
    total = lax.fori_loop(0, full, lambda t, c: step(t, c, False), total)
    total = lax.fori_loop(full, count, lambda t, c: step(t, c, True), total)
    dq_ref[...] = join_heads(total).astype(dq_ref.dtype)

    @pl.when(which == pl.num_programs(0) - 1)
    def _():
        def back(slot, _):
            target = pl.ds(pl.multiple_of(slot * block_rows, block_rows), block_rows)
            source = pl.ds(pl.multiple_of(table[slot] * block_rows, block_rows), block_rows)
            dk_ref[target, :] = dk_seq[source, :].astype(dk_ref.dtype)
            dv_ref[target, :] = dv_seq[source, :].astype(dv_ref.dtype)
            return 0

        lax.fori_loop(0, table.shape[0], back, 0)


STAT_LANES = 128


def attention_cost(length, rows, lanes, products):
    area = rows * length // 2
    return pl.CostEstimate(
        flops=products * 2 * area * lanes,
        bytes_accessed=8 * length * lanes,
        transcendentals=2 * area * lanes // HD,
    )


def attention_call(kernel, operands, dealt, mine, keys, values):
    back = len(operands) > 1
    rows, lanes = operands[0].shape
    length = keys.shape[0]
    blocks = mine.shape[0]
    block_rows = rows // blocks
    stacked = block_rows * lanes // HD
    small = pl.BlockSpec((block_rows, lanes), lambda b, *_: (b, 0))
    stats = pl.BlockSpec((1, stacked, STAT_LANES), lambda b, *_: (b, 0, 0))
    wide = pl.BlockSpec((length, lanes), lambda b, *_: (0, 0), pipeline_mode=pl.Buffered(1))
    if back:
        in_specs, out_specs = [small, small, small, stats, wide, wide], [small, wide, wide]
        grad = jax.ShapeDtypeStruct((length, lanes), jnp.bfloat16)
        out_shape = (jax.ShapeDtypeStruct((rows, lanes), jnp.bfloat16), grad, grad)
    else:
        in_specs, out_specs = [small, wide, wide], [small, stats]
        out_shape = (
            jax.ShapeDtypeStruct((rows, lanes), jnp.float32),
            jax.ShapeDtypeStruct((blocks, stacked, STAT_LANES), jnp.float32),
        )
    scratch = [pltpu.VMEM((length, lanes), jnp.bfloat16)] * 2
    if back:
        scratch = scratch + [pltpu.VMEM((length, lanes), jnp.float32)] * 2
    return pl.pallas_call(
        kernel,
        out_shape=out_shape,
        grid_spec=pltpu.PrefetchScalarGridSpec(
            num_scalar_prefetch=2,
            grid=(blocks,),
            in_specs=in_specs,
            out_specs=out_specs,
            scratch_shapes=scratch,
        ),
        compiler_params=pltpu.CompilerParams(vmem_limit_bytes=(44 if length <= 8192 else 58) << 20),
        cost_estimate=attention_cost(length, rows, lanes, 5 if back else 2),
    )(dealt, mine, *operands, keys, values)


def head_parts(length, lanes):
    width = lanes if length <= 8192 else HD
    return [slice(at, at + width) for at in range(0, lanes, width)]


def attend(queries, keys, values, dealt, mine):
    results = [
        attention_call(forward_kernel, (queries[:, p],), dealt, mine, keys[:, p], values[:, p])
        for p in head_parts(keys.shape[0], keys.shape[1])
    ]
    return jnp.concatenate([r[0] for r in results], 1), [r[1] for r in results]


def attend_back(queries, grads, attended, stats, keys, values, dealt, mine):
    results = []
    for p, stat in zip(head_parts(keys.shape[0], keys.shape[1]), stats):
        operands = (queries[:, p], grads[:, p], attended[:, p], stat)
        results.append(
            attention_call(backward_kernel, operands, dealt, mine, keys[:, p], values[:, p])
        )
    return [jnp.concatenate([r[i] for r in results], 1) for i in range(3)]


HEAD_GROUPS = 4


def near_groups():
    count = lax.axis_size("ctx")
    return [list(range(at, at + HEAD_GROUPS)) for at in range(0, count, HEAD_GROUPS)]


def far_groups():
    count = lax.axis_size("ctx")
    return [list(range(at, count, HEAD_GROUPS)) for at in range(HEAD_GROUPS)]


def to_heads(arrays):
    rows = arrays[0].shape[0]
    parts = [a.reshape(rows, HEAD_GROUPS, -1).transpose(1, 0, 2) for a in arrays]
    packed = parts[0] if len(parts) == 1 else jnp.concatenate(parts, 2)
    moved = lax.all_to_all(packed, "ctx", 0, 0, axis_index_groups=near_groups(), tiled=True)
    return moved.reshape(HEAD_GROUPS * rows, -1)


def to_tokens(packed, count):
    rows = packed.shape[0] // HEAD_GROUPS
    packed = packed.reshape(HEAD_GROUPS, rows, -1)
    moved = lax.all_to_all(packed, "ctx", 0, 0, axis_index_groups=near_groups(), tiled=True)
    moved = moved.reshape(HEAD_GROUPS, rows, count, -1).transpose(2, 1, 0, 3)
    return moved.reshape(count, rows, -1)


def gather_vectors(vectors):
    sizes = [v.shape[0] for v in vectors]
    both = lax.all_gather(jnp.concatenate(vectors), "shard", axis=0)
    out, at = [], 0
    for size in sizes:
        out.append(both[:, at : at + size].reshape(-1).astype(jnp.float32))
        at += size
    return out


def sum_vectors(vectors):
    halves = lax.axis_size("shard")
    sizes = [v.shape[0] // halves for v in vectors]
    packed = jnp.concatenate([v.reshape(halves, -1) for v in vectors], 1)
    summed = lax.psum(packed, ("ctx", "shard"))
    here = lax.dynamic_index_in_dim(summed, lax.axis_index("shard"), 0, keepdims=False)
    out, at = [], 0
    for size in sizes:
        out.append(here[at : at + size])
        at += size
    return out


def share_of(term):
    return lax.psum_scatter(term.astype(jnp.bfloat16), "shard", scatter_dimension=0, tiled=True)


def body(
    inputs,
    cotangent,
    block_table,
    first_gain,
    first_shift,
    query_weight,
    query_bias,
    keyvalue_weight,
    value_bias,
    out_weight,
    out_bias,
    second_gain,
    second_shift,
    up_weight,
    up_bias,
    down_weight,
    down_bias,
):
    my_index = lax.axis_index("ctx")
    dealt = block_table.reshape(-1)
    first_near = my_index // HEAD_GROUPS * HEAD_GROUPS
    mine = lax.dynamic_slice_in_dim(block_table, first_near, HEAD_GROUPS, 0).reshape(-1)
    model_width = inputs.shape[2]
    lanes = model_width // HEAD_GROUPS
    gain_one, shift_one, b_query, b_value, b_out, gain_two, shift_two, b_up, b_down = gather_vectors(
        [
            first_gain,
            first_shift,
            query_bias,
            value_bias,
            out_bias,
            second_gain,
            second_shift,
            up_bias,
            down_bias,
        ]
    )
    w_keyvalue = lax.all_gather(keyvalue_weight, "shard", axis=0, tiled=True)
    w_query = lax.all_gather(query_weight, "shard", axis=0, tiled=True)
    w_down = lax.all_gather(down_weight, "shard", axis=0, tiled=True)
    w_out = lax.all_gather(out_weight, "shard", axis=0, tiled=True)
    w_up = lax.all_gather(up_weight, "shard", axis=0, tiled=True)
    kv_shift = jnp.concatenate([jnp.zeros_like(b_value), b_value])
    hidden = inputs[0].astype(jnp.float32)
    normed = normalize(hidden, gain_one, shift_one).astype(jnp.bfloat16)
    kv_local = (matmul(normed, w_keyvalue) + kv_shift).astype(jnp.bfloat16)
    queries = ((matmul(normed, w_query) + b_query) * 0.125).astype(jnp.bfloat16)
    down_grad_in = cotangent[0]
    upstream = down_grad_in.astype(jnp.float32)
    dactive = times_transpose(down_grad_in, w_down)
    near = to_heads([queries, kv_local[:, :model_width], kv_local[:, model_width:]])
    near_queries = near[:, :lanes]
    kv_all = lax.all_gather(
        near[:, lanes:], "ctx", axis=0, axis_index_groups=far_groups(), tiled=True
    )
    near_keys, near_values = kv_all[:, :lanes], kv_all[:, lanes:]
    attended, stats = attend(near_queries, near_keys, near_values, dealt, mine)
    attended_low = to_tokens(attended.astype(jnp.bfloat16), 1)[0]
    middle = hidden + matmul(attended_low, w_out) + b_out
    second = normalize(middle, gain_two, shift_two).astype(jnp.bfloat16)
    pre_act = matmul(second, w_up) + b_up
    active = gelu_tanh(pre_act).astype(jnp.bfloat16)
    down_share = share_of(outer_sum(active, down_grad_in))
    _, gelu_pull = jax.vjp(gelu_tanh, pre_act)
    dpre = gelu_pull(dactive)[0].astype(jnp.bfloat16)
    up_share = share_of(outer_sum(second, dpre))
    result = middle + matmul(active, w_down) + b_down
    dsecond = times_transpose(dpre, w_up)
    _, norm_pull_two = jax.vjp(normalize, middle, gain_two, shift_two)
    dmiddle_part, dgain_two, dshift_two = norm_pull_two(dsecond)
    dmiddle = upstream + dmiddle_part
    dbranch = dmiddle.astype(jnp.bfloat16)
    dattended = times_transpose(dbranch, w_out).astype(jnp.bfloat16)
    out_share = share_of(outer_sum(attended_low, dbranch))
    early = lax.psum((down_share, up_share, out_share), "ctx")
    near_dq, near_dk, near_dv = attend_back(
        near_queries, to_heads([dattended]), attended, stats, near_keys, near_values, dealt, mine
    )
    near_dkv = lax.psum_scatter(
        jnp.concatenate([near_dk, near_dv], 1),
        "ctx",
        scatter_dimension=0,
        axis_index_groups=far_groups(),
        tiled=True,
    )
    dquery, dkey, dvalue = to_tokens(jnp.concatenate([near_dq, near_dkv], 1), 3)
    kv_grad_low = jnp.concatenate([dkey, dvalue], 1)
    late_shares = (
        share_of(outer_sum(normed, dquery) * 0.125),
        share_of(outer_sum(normed, kv_grad_low)),
    )
    early, late_shares = lax.optimization_barrier((early, late_shares))
    late = lax.psum(late_shares, "ctx")
    down_grad, up_grad, out_grad = (part.astype(jnp.float32) for part in early)
    query_grad, keyvalue_grad = (part.astype(jnp.float32) for part in late)
    dnormed = times_transpose(dquery, w_query) * 0.125 + times_transpose(kv_grad_low, w_keyvalue)
    _, norm_pull_one = jax.vjp(normalize, hidden, gain_one, shift_one)
    dhidden_part, dgain_one, dshift_one = norm_pull_one(dnormed)
    input_grad = (dmiddle + dhidden_part).astype(jnp.bfloat16)
    (
        gain_one_grad,
        shift_one_grad,
        query_bias_grad,
        value_bias_grad,
        out_bias_grad,
        gain_two_grad,
        shift_two_grad,
        up_bias_grad,
        down_bias_grad,
    ) = sum_vectors(
        [
            dgain_one,
            dshift_one,
            jnp.sum(dquery.astype(jnp.float32), 0) * 0.125,
            jnp.sum(dvalue.astype(jnp.float32), 0),
            jnp.sum(dbranch.astype(jnp.float32), 0),
            dgain_two,
            dshift_two,
            jnp.sum(dpre.astype(jnp.float32), 0),
            jnp.sum(upstream, 0),
        ]
    )
    return (
        result.astype(jnp.bfloat16)[None],
        input_grad[None],
        gain_one_grad,
        shift_one_grad,
        query_grad,
        query_bias_grad,
        keyvalue_grad,
        value_bias_grad,
        out_grad,
        out_bias_grad,
        gain_two_grad,
        shift_two_grad,
        up_grad,
        up_bias_grad,
        down_grad,
        down_bias_grad,
    )


def solution(mesh):
    in_specs = (
        P("shard", "ctx", None),
        P("shard", "ctx", None),
        P(),
        P("shard"),
        P("shard"),
        P("shard", None),
        P("shard"),
        P("shard", None),
        P("shard"),
        P("shard", None),
        P("shard"),
        P("shard"),
        P("shard"),
        P("shard", None),
        P("shard"),
        P("shard", None),
        P("shard"),
    )
    out_specs = (
        P("shard", "ctx", None),
        P("shard", "ctx", None),
        P("shard"),
        P("shard"),
        P("shard", None),
        P("shard"),
        P("shard", None),
        P("shard"),
        P("shard", None),
        P("shard"),
        P("shard"),
        P("shard"),
        P("shard", None),
        P("shard"),
        P("shard", None),
        P("shard"),
    )
    return jax.shard_map(body, mesh=mesh, in_specs=in_specs, out_specs=out_specs, check_vma=False)
```
